32 devices in a mesh: groups: 2 (over x), chan: 16 (over z, y, core).
Axes of the slice: x: 2, y: 2, z: 4, core: 2. Of those that a mesh axis runs over, the one named last changes fastest.
Arguments:
- maps: bfloat16 [4, 3072, 256], P('groups', 'chan'), parts along dimension 0, may hold values from -6 to 6
- kernels: bfloat16 [1, 9, 3072, 3072], P(None, None, 'chan'), may hold values from -0.0546875 to 0.0546875
- bias: float32 [1, 3072], P(None, 'chan'), may hold values from -3 to 3
Outputs:
- features: bfloat16 [4, 3072, 256], P('groups', 'chan'), parts along dimension 0
The draws below stay inside these ranges and needn't reach their ends.
There are 2 independent parts, one for each index of `groups`. The reference program is written for one: setup_inputs(seed, part) draws one part's arguments, and reference() takes and returns one part's arrays. A program takes and returns all parts, laid end to end along the dimension named above; an argument that names none is the same for every part. Nothing has to cross between parts.
All inputs are finite; a program needn't handle non-finite values.
Results may differ from the reference program's by a relative error of at most 0.0011.
Values may be sent and summed in bfloat16 or wider, within the bound.
No kernel may reach another device: no remote copies, remote signals or barrier semaphores. Data moves between devices by JAX's collectives and lax.ppermute only.
A program may use at most 64 MiB of HBM per device.

```python
import jax
import jax.numpy as jnp
from jax import lax

C = 3072
PIX = 256
MICRO = 2
LAYERS = 1


def spiked(array, stream_key, source, target, blocks, factor):
    def block_of(axis_at):
        return (jnp.arange(array.shape[axis_at]) // (array.shape[axis_at] // blocks)).reshape((-1,) + (1,) * (array.ndim - 1 - axis_at))

    near = jax.random.permutation(stream_key, blocks)[block_of(target)]
    second = (block_of(target) + blocks // 2) % blocks
    return jnp.where((block_of(source) == near) | (block_of(source) == second), factor * array, array)


def block_scale(key, shape, split, smallest, top_value):
    factor_of = 1.0
    for position, blocks in split:
        steps = jax.random.uniform(jax.random.fold_in(jax.random.fold_in(key, 6), position), (blocks,), jnp.float32, smallest / len(split), top_value / len(split))
        factor_of = factor_of * jnp.repeat(jnp.exp(steps), shape[position] // blocks).reshape((-1,) + (1,) * (len(shape) - 1 - position))
    return factor_of


def gaussian(stream_key, extent, spread, limit, split=(), kind=jnp.bfloat16):
    drawn = spread * jax.random.normal(stream_key, extent, jnp.float32)
    if split:
        drawn = drawn * block_scale(stream_key, extent, split, -0.22, 0.18)
    return jnp.clip(drawn, -limit, limit).astype(kind)


def heavy_noise(own_key, dims, spread, reach, split, heavy, held_as=jnp.bfloat16):
    values = spread * jax.random.normal(own_key, dims, jnp.float32)
    if split:
        values = values * block_scale(own_key, dims, split, -0.22, 0.18)
    return jnp.clip(spiked(values, jax.random.fold_in(own_key, 3), *heavy), -reach, reach).astype(held_as)


def setup_inputs(seed: int = 0, part: int = 0) -> dict:
    key_list = jax.random.split(jax.random.key(seed), 4)
    part_splits = jax.random.split(jax.random.fold_in(key_list[3], part), 4)
    maps = gaussian(part_splits[0], (MICRO, C, PIX), 1.0, 6.0, ((1, 16),))
    kernels = heavy_noise(key_list[1], (LAYERS, 9, C, C), (9 * C) ** -0.5, 0.0546875, ((2, 16),), (2, 3, 16, 2.0))
    bias = gaussian(key_list[2], (LAYERS, C), 0.5, 3.0, ((1, 16),), jnp.float32)
    return {"maps": maps, "kernels": kernels, "bias": bias}


def make_patches(stack):
    count = stack.shape[0]
    depth = stack.shape[1]
    images = stack.reshape(count, depth, 16, 16)
    padded = jnp.pad(images, ((0, 0), (0, 0), (1, 1), (1, 1)))
    shifted = [padded[:, :, row:row + 16, col:col + 16] for row in range(3) for col in range(3)]
    joined = jnp.stack(shifted, 0)
    return jnp.transpose(joined, (0, 2, 1, 3, 4)).reshape(9 * depth, count * 256)


def reference(maps, kernels, bias):
    results = []
    for micro in range(MICRO):
        state = maps[micro][None]
        for layer in range(LAYERS):
            columns = make_patches(state)
            flat = kernels[layer].reshape(9 * C, C)
            total = lax.dot_general(flat, columns, (((0,), (0,)), ((), ())), preferred_element_type=jnp.float32)
            updated = state[0].astype(jnp.float32) + jnp.maximum(total + bias[layer][:, None], 0.0)
            state = updated.astype(jnp.bfloat16)[None]
        results.append(state[0])
    return jnp.stack(results, 0)
```

```python
import functools
import math

import jax
import jax.numpy as jnp
from jax import lax
from jax.experimental import pallas as pl
from jax.experimental.pallas import tpu as pltpu
from jax.sharding import PartitionSpec as P

AXIS = "chan"
SENT = jnp.float16


def make_patches(stack):
    count, depth, pixels = stack.shape
    side = math.isqrt(pixels)
    images = stack.reshape(count, depth, side, side)
    padded = jnp.pad(images, ((0, 0), (0, 0), (1, 1), (1, 1)))
    shifted = [padded[:, :, row : row + side, col : col + side] for row in range(3) for col in range(3)]
    joined = jnp.stack(shifted, 0)
    return jnp.transpose(joined, (0, 2, 1, 3, 4)).reshape(9 * depth, count * pixels)


def finish(stack, total, layer_bias):
    count, owned, pixels = stack.shape
    activated = jnp.maximum(total + layer_bias[:, None], 0.0)
    activated = jnp.transpose(activated.reshape(owned, count, pixels), (1, 0, 2))
    return (stack.astype(jnp.float32) + activated).astype(jnp.bfloat16)


def conv_plain(stack, flat, layer_bias):
    columns = make_patches(stack)
    total = lax.psum_scatter(
        lax.dot_general(flat, columns, (((0,), (0,)), ((), ())), preferred_element_type=jnp.float32),
        AXIS,
        scatter_dimension=0,
        tiled=True,
    )
    return finish(stack, total, layer_bias)


def write_patches(maps_ref, x_ref):
    count, depth, pixels = maps_ref.shape
    side = math.isqrt(pixels)
    lane = lax.broadcasted_iota(jnp.int32, (depth, pixels), 1)
    row, col = lane // side, lane % side
    for m in range(count):
        image = maps_ref[m]
        wide = image.astype(jnp.float32)
        for tap in range(9):
            dy, dx = tap // 3 - 1, tap % 3 - 1
            shift = dy * side + dx
            value = image
            if shift:
                value = pltpu.roll(wide, (-shift) % pixels, 1)
                for step, place in ((dy, row), (dx, col)):
                    if step > 0:
                        value = jnp.where(place < side - 1, value, 0.0)
                    elif step < 0:
                        value = jnp.where(place > 0, value, 0.0)
                value = value.astype(jnp.bfloat16)
            x_ref[tap * depth : (tap + 1) * depth, m * pixels : (m + 1) * pixels] = value


def partial_kernel(m, first, source, w_ref, *refs):
    if first:
        x_ref, send_ref, keep_ref, w_buf, sem = refs
    else:
        send_ref, keep_ref, w_buf, sem = refs
        x_ref = source
    me = lax.axis_index(AXIS)
    low, pair = lax.rem(me, 2), lax.div(me, 2)
    width = w_buf.shape[2]
    owned = width // 2
    copies = []
    for j in (1, 0):
        start = pl.multiple_of((pair ^ (2 * m + j)) * width, 128)
        copy = pltpu.make_async_copy(w_ref.at[:, pl.ds(start, width)], w_buf.at[j], sem.at[j])
        copy.start()
        copies.append((j, copy))
    if first:
        write_patches(source, x_ref)
    for j, copy in copies:
        copy.wait()
        part = lax.dot_general(
            w_buf[j], x_ref[...], (((0,), (0,)), ((), ())), preferred_element_type=jnp.float32
        )

        @pl.when(low == 0)
        def _():
            keep_ref[j] = part[:owned]
            send_ref[j] = part[owned:]

        @pl.when(low == 1)
        def _():
            keep_ref[j] = part[owned:]
            send_ref[j] = part[:owned]


def partials(m, first, source, flat, owned, columns):
    depth = flat.shape[0]
    vmem = pl.BlockSpec(memory_space=pltpu.VMEM)
    half = jax.ShapeDtypeStruct((2, owned, columns), jnp.float32)
    patches = jax.ShapeDtypeStruct((depth, columns), jnp.bfloat16)
    return pl.pallas_call(
        functools.partial(partial_kernel, m, first),
        in_specs=[vmem, pl.BlockSpec(memory_space=pltpu.HBM)],
        out_specs=[vmem] * (3 if first else 2),
        out_shape=([patches] if first else []) + [half, half],
        scratch_shapes=[pltpu.VMEM((2, depth, 2 * owned), jnp.bfloat16), pltpu.SemaphoreType.DMA((2,))],
        compiler_params=pltpu.CompilerParams(vmem_limit_bytes=32 * 2**20),
        cost_estimate=pl.CostEstimate(
            flops=2 * depth * 4 * owned * columns,
            bytes_accessed=2 * depth * 4 * owned,
            transcendentals=0,
        ),
        name=f"partials_{m}",
    )(source, flat)


def conv_halving(stack, flat, layer_bias, size):
    count, owned, pixels = stack.shape
    columns = count * pixels

    def swap(value, bit):
        return lax.ppermute(value, AXIS, [(i, i ^ bit) for i in range(size)])

    chunks = size // 4
    sums = {}
    patches = None
    for m in reversed(range(chunks)):
        if patches is None:
            patches, send, keep = partials(m, True, stack, flat, owned, columns)
        else:
            send, keep = partials(m, False, patches, flat, owned, columns)
        came = swap(send, 1)
        second = swap((keep[1] + came[1]).astype(SENT), 2)
        sums[m] = keep[0] + came[0] + second.astype(jnp.float32)
    bit = 1
    while bit < chunks:
        for m in reversed(range(chunks)):
            if m % bit == 0 and m & bit:
                came = swap(sums[m].astype(SENT), 4 * bit)
                sums[m - bit] = sums[m - bit] + came.astype(jnp.float32)
        bit *= 2
    return finish(stack, sums[0], layer_bias)


def local(size, maps, kernels, bias):
    for layer in range(kernels.shape[0]):
        owned = maps.shape[1]
        flat = kernels[layer].reshape(9 * owned, kernels.shape[3])
        if size >= 4 and size & (size - 1) == 0 and owned % 64 == 0 and maps.shape[2] % 128 == 0:
            maps = conv_halving(maps, flat, bias[layer], size)
        else:
            maps = conv_plain(maps, flat, bias[layer])
    return maps


def solution(mesh):
    in_specs = (P("groups", AXIS, None), P(None, None, AXIS, None), P(None, AXIS))
    out_specs = P("groups", AXIS, None)
    return jax.shard_map(
        functools.partial(local, mesh.shape[AXIS]), mesh=mesh, in_specs=in_specs, out_specs=out_specs, check_vma=False
    )
```

```python
import functools
import math

import jax
import jax.numpy as jnp
from jax import lax
from jax.experimental import pallas as pl
from jax.experimental.pallas import tpu as pltpu
from jax.sharding import PartitionSpec as P

AXIS = "chan"
SENT = jnp.float16


def make_patches(stack):
    count, depth, pixels = stack.shape
    side = math.isqrt(pixels)
    images = stack.reshape(count, depth, side, side)
    padded = jnp.pad(images, ((0, 0), (0, 0), (1, 1), (1, 1)))
    shifted = [padded[:, :, row : row + side, col : col + side] for row in range(3) for col in range(3)]
    joined = jnp.stack(shifted, 0)
    return jnp.transpose(joined, (0, 2, 1, 3, 4)).reshape(9 * depth, count * pixels)


def conv_plain(stack, flat, layer_bias):
    count, owned, pixels = stack.shape
    total = lax.psum_scatter(
        lax.dot_general(flat, make_patches(stack), (((0,), (0,)), ((), ())), preferred_element_type=jnp.float32),
        AXIS,
        scatter_dimension=0,
        tiled=True,
    )
    activated = jnp.maximum(total + layer_bias[:, None], 0.0)
    activated = jnp.transpose(activated.reshape(owned, count, pixels), (1, 0, 2))
    return (stack.astype(jnp.float32) + activated).astype(jnp.bfloat16)


def write_patches(maps_ref, x_ref):
    count, depth, pixels = maps_ref.shape
    side = math.isqrt(pixels)
    lane = lax.broadcasted_iota(jnp.int32, (depth, pixels), 1)
    row, col = lane // side, lane % side
    for image in range(count):
        plain = maps_ref[image]
        wide = plain.astype(jnp.float32)
        for tap in range(9):
            dy, dx = tap // 3 - 1, tap % 3 - 1
            shift = dy * side + dx
            value = plain
            if shift:
                value = pltpu.roll(wide, (-shift) % pixels, 1)
                for step, place in ((dy, row), (dx, col)):
                    if step > 0:
                        value = jnp.where(place < side - 1, value, 0.0)
                    elif step < 0:
                        value = jnp.where(place > 0, value, 0.0)
                value = value.astype(jnp.bfloat16)
            x_ref[tap * depth : (tap + 1) * depth, image * pixels : (image + 1) * pixels] = value


def contribution(x_ref, weights, low, out_ref):
    _, count, owned, pixels = out_ref.shape
    part = lax.dot_general(weights, x_ref[...], (((0,), (0,)), ((), ())), preferred_element_type=jnp.float32)
    for core in range(2):
        for image in range(count):
            rows, at = slice(core * owned, (core + 1) * owned), slice(image * pixels, (image + 1) * pixels)
            out_ref[low ^ core, image] = part[rows, at]


def columns_of(distance, width):
    pair = lax.div(lax.axis_index(AXIS), 2)
    return pl.ds(pl.multiple_of((pair ^ distance) * width, 128), width)


def first_kernel(distances, maps_ref, w_ref, x_ref, out_ref, maps_buf, w_buf, sems):
    low = lax.rem(lax.axis_index(AXIS), 2)
    maps_copy = pltpu.make_async_copy(maps_ref, maps_buf, sems.at[0])
    maps_copy.start()
    copies = []
    for at, distance in enumerate(distances):
        columns = columns_of(distance, w_buf.shape[2])
        copies.append(pltpu.make_async_copy(w_ref.at[:, columns], w_buf.at[at], sems.at[1 + at]))
        copies[-1].start()
    maps_copy.wait()
    write_patches(maps_buf, x_ref)
    for at, copy in enumerate(copies):
        copy.wait()
        contribution(x_ref, w_buf[at], low, out_ref.at[:, at])


def next_kernel(distances, x_ref, w_ref, out_ref):
    low = lax.rem(lax.axis_index(AXIS), 2)
    width = 2 * out_ref.shape[3]
    for at, distance in enumerate(distances):
        contribution(x_ref, w_ref[:, columns_of(distance, width)], low, out_ref.at[:, at])


def partials(distances, source, flat, shape, first=False):
    count, owned, pixels = shape
    depth = flat.shape[0]
    sums = jax.ShapeDtypeStruct((2, len(distances), count, owned, pixels), jnp.float32)
    patches = jax.ShapeDtypeStruct((depth, count * pixels), jnp.bfloat16)
    vmem, hbm = pl.BlockSpec(memory_space=pltpu.VMEM), pl.BlockSpec(memory_space=pltpu.HBM)
    scratch = []
    if first:
        source = pltpu.with_memory_space_constraint(source, pltpu.HBM)
        flat = pltpu.with_memory_space_constraint(flat, pltpu.HBM)
        scratch = [
            pltpu.VMEM(shape, jnp.bfloat16),
            pltpu.VMEM((len(distances), depth, 2 * owned), jnp.bfloat16),
            pltpu.SemaphoreType.DMA((1 + len(distances),)),
        ]
    return pl.pallas_call(
        functools.partial(first_kernel if first else next_kernel, distances),
        in_specs=[hbm, hbm] if first else [vmem, vmem],
        out_specs=[vmem] * 2 if first else vmem,
        out_shape=[patches, sums] if first else sums,
        scratch_shapes=scratch,
        compiler_params=pltpu.CompilerParams(vmem_limit_bytes=24 * 2**20),
        cost_estimate=pl.CostEstimate(
            flops=4 * depth * len(distances) * owned * count * pixels,
            bytes_accessed=4 * depth * len(distances) * owned,
            transcendentals=0,
        ),
        name="partials_" + "_".join(map(str, distances)),
    )(source, flat)


def conv_halving(stack, flat, layer_bias):
    shape = stack.shape
    images = range(shape[0])
    size = lax.axis_size(AXIS)

    def swap(value, bits):
        return lax.ppermute(value, AXIS, [(i, i ^ bits) for i in range(size)])

    def wide(value):
        return value.astype(jnp.float32)

    def core_sums(distances, out):
        came = swap(out[1].astype(SENT), 1)
        return {d: [out[0, at, i] + wide(came[at, i]) for i in images] for at, d in enumerate(distances)}

    def across(sums, distance):
        return swap(jnp.stack([value.astype(SENT) for value in sums]), 2 * distance)

    far, near = (7, 6, 5, 4), (3, 2, 1, 0)
    patches, out = partials(far, stack, flat, shape, first=True)
    later = partials(near, patches, flat, shape)
    sums = core_sums(far, out)
    came = [across(sums[d], d - 4) for d in (5, 6, 7)]
    kept = [sums[4][i] + sum(wide(c[i]) for c in came) for i in images]
    sums = core_sums(near, later)
    came = [across(sums[d], d) for d in (1, 2, 3)]
    came.append(across(kept, 4))
    bias = layer_bias[:, None]
    total = [sums[0][i] + sum(wide(c[i]) for c in came) for i in images]
    return jnp.stack([(wide(stack[i]) + jnp.maximum(total[i] + bias, 0.0)).astype(jnp.bfloat16) for i in images])


def local(size, maps, kernels, bias):
    for layer in range(kernels.shape[0]):
        owned = maps.shape[1]
        flat = kernels[layer].reshape(9 * owned, kernels.shape[3])
        if size == 16 and owned % 64 == 0 and maps.shape[2] % 128 == 0:
            maps = conv_halving(maps, flat, bias[layer])
        else:
            maps = conv_plain(maps, flat, bias[layer])
    return maps


def solution(mesh):
    in_specs = (P("groups", AXIS, None), P(None, None, AXIS, None), P(None, AXIS))
    out_specs = P("groups", AXIS, None)
    return jax.shard_map(
        functools.partial(local, mesh.shape[AXIS]), mesh=mesh, in_specs=in_specs, out_specs=out_specs, check_vma=False
    )
```

```python
import functools
import math

import jax
import jax.numpy as jnp
from jax import lax
from jax.experimental import pallas as pl
from jax.experimental.pallas import tpu as pltpu
from jax.sharding import PartitionSpec as P

AXIS = "chan"
SENT = jnp.float16


def make_patches(stack):
    count, depth, pixels = stack.shape
    side = math.isqrt(pixels)
    images = stack.reshape(count, depth, side, side)
    padded = jnp.pad(images, ((0, 0), (0, 0), (1, 1), (1, 1)))
    shifted = [padded[:, :, row : row + side, col : col + side] for row in range(3) for col in range(3)]
    joined = jnp.stack(shifted, 0)
    return jnp.transpose(joined, (0, 2, 1, 3, 4)).reshape(9 * depth, count * pixels)


def conv_plain(stack, flat, layer_bias):
    count, owned, pixels = stack.shape
    total = lax.psum_scatter(
        lax.dot_general(flat, make_patches(stack), (((0,), (0,)), ((), ())), preferred_element_type=jnp.float32),
        AXIS,
        scatter_dimension=0,
        tiled=True,
    )
    activated = jnp.maximum(total + layer_bias[:, None], 0.0)
    activated = jnp.transpose(activated.reshape(owned, count, pixels), (1, 0, 2))
    return (stack.astype(jnp.float32) + activated).astype(jnp.bfloat16)


def write_patches(maps_ref, x_ref):
    count, depth, pixels = maps_ref.shape
    side = math.isqrt(pixels)
    lane = lax.broadcasted_iota(jnp.int32, (depth, pixels), 1)
    row, col = lane // side, lane % side
    for image in range(count):
        plain = maps_ref[image]
        wide = plain.astype(jnp.float32)
        for tap in range(9):
            dy, dx = tap // 3 - 1, tap % 3 - 1
            shift = dy * side + dx
            value = plain
            if shift:
                value = pltpu.roll(wide, (-shift) % pixels, 1)
                for step, place in ((dy, row), (dx, col)):
                    if step > 0:
                        value = jnp.where(place < side - 1, value, 0.0)
                    elif step < 0:
                        value = jnp.where(place > 0, value, 0.0)
                value = value.astype(jnp.bfloat16)
            x_ref[tap * depth : (tap + 1) * depth, image * pixels : (image + 1) * pixels] = value


def contribution(x_ref, weights, low, out_ref):
    _, count, owned, pixels = out_ref.shape
    part = lax.dot_general(weights, x_ref[...], (((0,), (0,)), ((), ())), preferred_element_type=jnp.float32)
    for core in range(2):
        for image in range(count):
            rows, at = slice(core * owned, (core + 1) * owned), slice(image * pixels, (image + 1) * pixels)
            out_ref[low ^ core, image] = part[rows, at]


def columns_of(distance, width):
    pair = lax.div(lax.axis_index(AXIS), 2)
    return pl.ds(pl.multiple_of((pair ^ distance) * width, 128), width)


def first_kernel(distances, rest, maps_ref, w_ref, x_ref, out_ref, rest_ref, maps_buf, w_buf, sems):
    low = lax.rem(lax.axis_index(AXIS), 2)
    maps_copy = pltpu.make_async_copy(maps_ref, maps_buf, sems.at[0])
    maps_copy.start()
    copies = []
    for at, distance in enumerate(distances + rest):
        columns = columns_of(distance, w_buf.shape[2])
        target = w_buf.at[at] if at < len(distances) else rest_ref.at[at - len(distances)]
        copies.append(pltpu.make_async_copy(w_ref.at[:, columns], target, sems.at[1 + at]))
        copies[-1].start()
    maps_copy.wait()
    write_patches(maps_buf, x_ref)
    for at, copy in enumerate(copies[: len(distances)]):
        copy.wait()
        contribution(x_ref, w_buf[at], low, out_ref.at[:, at])
    for copy in copies[len(distances) :]:
        copy.wait()


def next_kernel(x_ref, w_ref, before_ref, after_ref, out_ref):
    low = lax.rem(lax.axis_index(AXIS), 2)
    for at in range(w_ref.shape[0]):
        contribution(x_ref, w_ref[at], low, out_ref.at[:, at])


def kernel_cost(depth, shape, chunks):
    count, owned, pixels = shape
    return pl.CostEstimate(
        flops=4 * depth * chunks * owned * count * pixels, bytes_accessed=4 * depth * chunks * owned, transcendentals=0
    )


def first_partials(distances, rest, stack, flat):
    count, owned, pixels = stack.shape
    depth = flat.shape[0]
    vmem, hbm = pl.BlockSpec(memory_space=pltpu.VMEM), pl.BlockSpec(memory_space=pltpu.HBM)
    return pl.pallas_call(
        functools.partial(first_kernel, distances, rest),
        in_specs=[hbm, hbm],
        out_specs=[vmem] * 3,
        out_shape=[
            jax.ShapeDtypeStruct((depth, count * pixels), jnp.bfloat16),
            jax.ShapeDtypeStruct((2, len(distances), *stack.shape), jnp.float32),
            jax.ShapeDtypeStruct((len(rest), depth, 2 * owned), jnp.bfloat16),
        ],
        scratch_shapes=[
            pltpu.VMEM(stack.shape, jnp.bfloat16),
            pltpu.VMEM((len(distances), depth, 2 * owned), jnp.bfloat16),
            pltpu.SemaphoreType.DMA((1 + len(distances) + len(rest),)),
        ],
        compiler_params=pltpu.CompilerParams(vmem_limit_bytes=24 * 2**20),
        cost_estimate=kernel_cost(depth, stack.shape, len(distances)),
        name="far_partials",
    )(pltpu.with_memory_space_constraint(stack, pltpu.HBM), pltpu.with_memory_space_constraint(flat, pltpu.HBM))


def next_partials(patches, weights, before, after, shape):
    vmem, unread = pl.BlockSpec(memory_space=pltpu.VMEM), pl.BlockSpec(memory_space=pl.ANY)
    return pl.pallas_call(
        next_kernel,
        in_specs=[vmem, vmem, unread, unread],
        out_specs=vmem,
        out_shape=jax.ShapeDtypeStruct((2, weights.shape[0], *shape), jnp.float32),
        compiler_params=pltpu.CompilerParams(vmem_limit_bytes=24 * 2**20),
        cost_estimate=kernel_cost(patches.shape[0], shape, weights.shape[0]),
        name="near_partials",
    )(patches, weights, before, after)


def conv_halving(stack, flat, layer_bias):
    shape = stack.shape
    images = range(shape[0])
    size = lax.axis_size(AXIS)

    def swap(value, bits):
        return lax.ppermute(value, AXIS, [(i, i ^ bits) for i in range(size)])

    def wide(value):
        return value.astype(jnp.float32)

    def core_sums(distances, parts, out):
        sums = {}
        for part in parts:
            first = distances.index(part[0])
            came = swap(out[1, first : first + len(part)].astype(SENT), 1)
            for k, d in enumerate(part):
                sums[d] = [out[0, first + k, i] + wide(came[k, i]) for i in images]
        return sums

    def across(sums, bit):
        came = swap(jnp.stack([value.astype(SENT) for value in sums]), 2 * bit)
        return [wide(came[i]) for i in images]

    def plus(sums, *others):
        for other in others:
            sums = [a + b for a, b in zip(sums, other)]
        return sums

    far, near = (7, 6, 5, 4), (3, 1, 2, 0)
    patches, out, weights = first_partials(far, near, stack, flat)
    sums = core_sums(far, (far,), out)
    near_out = next_partials(patches, weights, out, sums[7][0], shape)
    sums.update(core_sums(near, ((3,), (1, 2), (0,)), near_out))
    came5 = across(sums[5], 1)
    came6 = across(plus(sums[6], across(sums[7], 1)), 2)
    came4 = across(plus(sums[4], came5, came6), 4)
    came2 = across(plus(sums[2], across(sums[3], 1)), 2)
    came1 = across(sums[1], 1)
    total = plus(sums[0], came4, came2, came1)
    bias = layer_bias[:, None]
    return jnp.stack([(wide(stack[i]) + jnp.maximum(total[i] + bias, 0.0)).astype(jnp.bfloat16) for i in images])


def local(size, maps, kernels, bias):
    for layer in range(kernels.shape[0]):
        owned = maps.shape[1]
        flat = kernels[layer].reshape(9 * owned, kernels.shape[3])
        if size == 16 and owned % 64 == 0 and maps.shape[2] % 128 == 0:
            maps = conv_halving(maps, flat, bias[layer])
        else:
            maps = conv_plain(maps, flat, bias[layer])
    return maps


def solution(mesh):
    in_specs = (P("groups", AXIS, None), P(None, None, AXIS, None), P(None, AXIS))
    out_specs = P("groups", AXIS, None)
    return jax.shard_map(
        functools.partial(local, mesh.shape[AXIS]), mesh=mesh, in_specs=in_specs, out_specs=out_specs, check_vma=False
    )
```

```python
import functools
import math

import jax
import jax.numpy as jnp
from jax import lax
from jax.experimental import pallas as pl
from jax.experimental.pallas import tpu as pltpu
from jax.sharding import PartitionSpec as P

AXIS = "chan"
SENT = jnp.float16


def make_patches(stack):
    count, depth, pixels = stack.shape
    side = math.isqrt(pixels)
    images = stack.reshape(count, depth, side, side)
    padded = jnp.pad(images, ((0, 0), (0, 0), (1, 1), (1, 1)))
    shifted = [padded[:, :, row : row + side, col : col + side] for row in range(3) for col in range(3)]
    joined = jnp.stack(shifted, 0)
    return jnp.transpose(joined, (0, 2, 1, 3, 4)).reshape(9 * depth, count * pixels)


def conv_plain(stack, flat, layer_bias):
    count, owned, pixels = stack.shape
    total = lax.psum_scatter(
        lax.dot_general(flat, make_patches(stack), (((0,), (0,)), ((), ())), preferred_element_type=jnp.float32),
        AXIS,
        scatter_dimension=0,
        tiled=True,
    )
    activated = jnp.maximum(total + layer_bias[:, None], 0.0)
    activated = jnp.transpose(activated.reshape(owned, count, pixels), (1, 0, 2))
    return (stack.astype(jnp.float32) + activated).astype(jnp.bfloat16)


def write_patches(maps_ref, x_ref):
    count, depth, pixels = maps_ref.shape
    side = math.isqrt(pixels)
    lane = lax.broadcasted_iota(jnp.int32, (depth, pixels), 1)
    row, col = lane // side, lane % side
    for image in range(count):
        plain = maps_ref[image]
        wide = plain.astype(jnp.float32)
        for tap in range(9):
            dy, dx = tap // 3 - 1, tap % 3 - 1
            shift = dy * side + dx
            value = plain
            if shift:
                value = pltpu.roll(wide, (-shift) % pixels, 1)
                for step, place in ((dy, row), (dx, col)):
                    if step > 0:
                        value = jnp.where(place < side - 1, value, 0.0)
                    elif step < 0:
                        value = jnp.where(place > 0, value, 0.0)
                value = value.astype(jnp.bfloat16)
            x_ref[tap * depth : (tap + 1) * depth, image * pixels : (image + 1) * pixels] = value


def contribution(x_ref, weights, low, out_ref):
    _, count, owned, pixels = out_ref.shape
    part = lax.dot_general(weights, x_ref[...], (((0,), (0,)), ((), ())), preferred_element_type=jnp.float32)
    for core in range(2):
        for image in range(count):
            rows, at = slice(core * owned, (core + 1) * owned), slice(image * pixels, (image + 1) * pixels)
            out_ref[low ^ core, image] = part[rows, at]


def columns_of(distance, width):
    pair = lax.div(lax.axis_index(AXIS), 2)
    return pl.ds(pl.multiple_of((pair ^ distance) * width, 128), width)


def first_kernel(distances, rest, maps_ref, w_ref, x_ref, out_ref, rest_ref, maps_buf, w_buf, sems):
    low = lax.rem(lax.axis_index(AXIS), 2)
    maps_copy = pltpu.make_async_copy(maps_ref, maps_buf, sems.at[0])
    maps_copy.start()
    copies = []
    for at, distance in enumerate(distances + rest):
        columns = columns_of(distance, w_buf.shape[2])
        target = w_buf.at[at] if at < len(distances) else rest_ref.at[at - len(distances)]
        copies.append(pltpu.make_async_copy(w_ref.at[:, columns], target, sems.at[1 + at]))
        copies[-1].start()
    maps_copy.wait()
    write_patches(maps_buf, x_ref)
    for at, copy in enumerate(copies[: len(distances)]):
        copy.wait()
        contribution(x_ref, w_buf[at], low, out_ref.at[:, at])
    for copy in copies[len(distances) :]:
        copy.wait()


def next_kernel(first, x_ref, w_ref, *refs):
    out_ref = refs[-1]
    low = lax.rem(lax.axis_index(AXIS), 2)
    for at in range(out_ref.shape[1]):
        contribution(x_ref, w_ref[first + at], low, out_ref.at[:, at])


def kernel_cost(depth, shape, chunks):
    count, owned, pixels = shape
    return pl.CostEstimate(
        flops=4 * depth * chunks * owned * count * pixels, bytes_accessed=4 * depth * chunks * owned, transcendentals=0
    )


def first_partials(distances, rest, stack, flat):
    count, owned, pixels = stack.shape
    depth = flat.shape[0]
    vmem, hbm = pl.BlockSpec(memory_space=pltpu.VMEM), pl.BlockSpec(memory_space=pltpu.HBM)
    return pl.pallas_call(
        functools.partial(first_kernel, distances, rest),
        in_specs=[hbm, hbm],
        out_specs=[vmem] * 3,
        out_shape=[
            jax.ShapeDtypeStruct((depth, count * pixels), jnp.bfloat16),
            jax.ShapeDtypeStruct((2, len(distances), *stack.shape), jnp.float32),
            jax.ShapeDtypeStruct((len(rest), depth, 2 * owned), jnp.bfloat16),
        ],
        scratch_shapes=[
            pltpu.VMEM(stack.shape, jnp.bfloat16),
            pltpu.VMEM((len(distances), depth, 2 * owned), jnp.bfloat16),
            pltpu.SemaphoreType.DMA((1 + len(distances) + len(rest),)),
        ],
        compiler_params=pltpu.CompilerParams(vmem_limit_bytes=24 * 2**20),
        cost_estimate=kernel_cost(depth, stack.shape, len(distances)),
        name="partials_and_patches",
    )(pltpu.with_memory_space_constraint(stack, pltpu.HBM), pltpu.with_memory_space_constraint(flat, pltpu.HBM))


def next_partials(patches, weights, first, chunks, shape, before):
    vmem, unread = pl.BlockSpec(memory_space=pltpu.VMEM), pl.BlockSpec(memory_space=pl.ANY)
    return pl.pallas_call(
        functools.partial(next_kernel, first),
        in_specs=[vmem, vmem] + [unread] * len(before),
        out_specs=vmem,
        out_shape=jax.ShapeDtypeStruct((2, chunks, *shape), jnp.float32),
        compiler_params=pltpu.CompilerParams(vmem_limit_bytes=24 * 2**20),
        cost_estimate=kernel_cost(patches.shape[0], shape, chunks),
        name="partials_" + str(first),
    )(patches, weights, *before)


def conv_halving(stack, flat, layer_bias):
    shape = stack.shape
    images = range(shape[0])
    size = lax.axis_size(AXIS)

    def swap(value, bits):
        return lax.ppermute(value, AXIS, [(i, i ^ bits) for i in range(size)])

    def wide(value):
        return value.astype(jnp.float32)

    def core_sums(distances, parts, out):
        sums = {}
        for part in parts:
            first = distances.index(part[0])
            came = swap(out[1, first : first + len(part)].astype(SENT), 1)
            for k, d in enumerate(part):
                sums[d] = [out[0, first + k, i] + wide(came[k, i]) for i in images]
        return sums

    def across(sums, bit):
        came = swap(jnp.stack([value.astype(SENT) for value in sums]), 2 * bit)
        return [wide(came[i]) for i in images]

    def plus(sums, *others):
        for other in others:
            sums = [a + b for a, b in zip(sums, other)]
        return sums

    odd, even, near = (7, 5), (6, 4), (3, 1, 2, 0)
    patches, odd_out, weights = first_partials(odd, even + near, stack, flat)
    even_out = next_partials(patches, weights, 0, len(even), shape, (odd_out,))
    sums = core_sums(odd, (odd,), odd_out)
    sums.update(core_sums(even, (even,), even_out))
    near_out = next_partials(patches, weights, len(even), len(near), shape, (even_out, sums[7][0]))
    sums.update(core_sums(near, ((3,), (1, 2), (0,)), near_out))
    came5 = across(sums[5], 1)
    came6 = across(plus(sums[6], across(sums[7], 1)), 2)
    came4 = across(plus(sums[4], came5, came6), 4)
    came2 = across(plus(sums[2], across(sums[3], 1)), 2)
    came1 = across(sums[1], 1)
    total = plus(sums[0], came4, came2, came1)
    bias = layer_bias[:, None]
    return jnp.stack([(wide(stack[i]) + jnp.maximum(total[i] + bias, 0.0)).astype(jnp.bfloat16) for i in images])


def local(size, maps, kernels, bias):
    for layer in range(kernels.shape[0]):
        owned = maps.shape[1]
        flat = kernels[layer].reshape(9 * owned, kernels.shape[3])
        if size == 16 and owned % 64 == 0 and maps.shape[2] % 128 == 0:
            maps = conv_halving(maps, flat, bias[layer])
        else:
            maps = conv_plain(maps, flat, bias[layer])
    return maps


def solution(mesh):
    in_specs = (P("groups", AXIS, None), P(None, None, AXIS, None), P(None, AXIS))
    out_specs = P("groups", AXIS, None)
    return jax.shard_map(
        functools.partial(local, mesh.shape[AXIS]), mesh=mesh, in_specs=in_specs, out_specs=out_specs, check_vma=False
    )
```

```python
import functools
import math

import jax
import jax.numpy as jnp
from jax import lax
from jax.experimental import pallas as pl
from jax.experimental.pallas import tpu as pltpu
from jax.sharding import PartitionSpec as P

AXIS = "chan"
SENT = jnp.float16


def make_patches(stack):
    count, depth, pixels = stack.shape
    side = math.isqrt(pixels)
    images = stack.reshape(count, depth, side, side)
    padded = jnp.pad(images, ((0, 0), (0, 0), (1, 1), (1, 1)))
    shifted = [padded[:, :, row : row + side, col : col + side] for row in range(3) for col in range(3)]
    joined = jnp.stack(shifted, 0)
    return jnp.transpose(joined, (0, 2, 1, 3, 4)).reshape(9 * depth, count * pixels)


def conv_plain(stack, flat, layer_bias):
    count, owned, pixels = stack.shape
    total = lax.psum_scatter(
        lax.dot_general(flat, make_patches(stack), (((0,), (0,)), ((), ())), preferred_element_type=jnp.float32),
        AXIS,
        scatter_dimension=0,
        tiled=True,
    )
    activated = jnp.maximum(total + layer_bias[:, None], 0.0)
    activated = jnp.transpose(activated.reshape(owned, count, pixels), (1, 0, 2))
    return (stack.astype(jnp.float32) + activated).astype(jnp.bfloat16)


def write_patches(maps_ref, x_ref):
    count, depth, pixels = maps_ref.shape
    side = math.isqrt(pixels)
    lane = lax.broadcasted_iota(jnp.int32, (depth, pixels), 1)
    row, col = lane // side, lane % side
    for image in range(count):
        plain = maps_ref[image]
        wide = plain.astype(jnp.float32)
        for tap in range(9):
            dy, dx = tap // 3 - 1, tap % 3 - 1
            shift = dy * side + dx
            value = plain
            if shift:
                value = pltpu.roll(wide, (-shift) % pixels, 1)
                for step, place in ((dy, row), (dx, col)):
                    if step > 0:
                        value = jnp.where(place < side - 1, value, 0.0)
                    elif step < 0:
                        value = jnp.where(place > 0, value, 0.0)
                value = value.astype(jnp.bfloat16)
            x_ref[tap * depth : (tap + 1) * depth, image * pixels : (image + 1) * pixels] = value


def contribution(x_ref, weights, low, out_ref):
    _, count, owned, pixels = out_ref.shape
    part = lax.dot_general(weights, x_ref[...], (((0,), (0,)), ((), ())), preferred_element_type=jnp.float32)
    for core in range(2):
        for image in range(count):
            rows, at = slice(core * owned, (core + 1) * owned), slice(image * pixels, (image + 1) * pixels)
            out_ref[low ^ core, image] = part[rows, at]


def weights_of(w_ref, distance, width):
    pair = lax.div(lax.axis_index(AXIS), 2)
    start = pl.multiple_of(lax.rem(pair ^ distance, 2) * width, 128)
    return w_ref[w_ref.shape[0] - 1 - distance // 2, :, pl.ds(start, width)]


def first_kernel(distances, maps_ref, flat_ref, x_ref, out_ref, w_ref, maps_buf, sems):
    me = lax.axis_index(AXIS)
    low, block = lax.rem(me, 2), lax.div(me, 4)
    maps_copy = pltpu.make_async_copy(maps_ref, maps_buf, sems.at[w_ref.shape[0]])
    maps_copy.start()
    width = w_ref.shape[2]
    copies = []
    for at in range(w_ref.shape[0]):
        start = pl.multiple_of((block ^ (w_ref.shape[0] - 1 - at)) * width, 128)
        copies.append(pltpu.make_async_copy(flat_ref.at[:, pl.ds(start, width)], w_ref.at[at], sems.at[at]))
        copies[-1].start()
    maps_copy.wait()
    write_patches(maps_buf, x_ref)
    for at, distance in enumerate(distances):
        copies[at].wait()
        contribution(x_ref, weights_of(w_ref, distance, width // 2), low, out_ref.at[:, at])
    for copy in copies[len(distances) :]:
        copy.wait()


def next_kernel(distances, x_ref, w_ref, *refs):
    out_ref = refs[-1]
    low = lax.rem(lax.axis_index(AXIS), 2)
    for at, distance in enumerate(distances):
        contribution(x_ref, weights_of(w_ref, distance, w_ref.shape[2] // 2), low, out_ref.at[:, at])


def kernel_cost(depth, shape, chunks):
    count, owned, pixels = shape
    return pl.CostEstimate(
        flops=4 * depth * chunks * owned * count * pixels, bytes_accessed=4 * depth * chunks * owned, transcendentals=0
    )


def first_partials(distances, stack, flat):
    count, owned, pixels = stack.shape
    depth, width = flat.shape[0], 4 * owned
    blocks = flat.shape[1] // width
    vmem, hbm = pl.BlockSpec(memory_space=pltpu.VMEM), pl.BlockSpec(memory_space=pltpu.HBM)
    return pl.pallas_call(
        functools.partial(first_kernel, distances),
        in_specs=[hbm, hbm],
        out_specs=[vmem] * 3,
        out_shape=[
            jax.ShapeDtypeStruct((depth, count * pixels), jnp.bfloat16),
            jax.ShapeDtypeStruct((2, len(distances), *stack.shape), jnp.float32),
            jax.ShapeDtypeStruct((blocks, depth, width), jnp.bfloat16),
        ],
        scratch_shapes=[pltpu.VMEM(stack.shape, jnp.bfloat16), pltpu.SemaphoreType.DMA((blocks + 1,))],
        compiler_params=pltpu.CompilerParams(vmem_limit_bytes=24 * 2**20),
        cost_estimate=kernel_cost(depth, stack.shape, len(distances)),
        name="partials_and_patches",
    )(pltpu.with_memory_space_constraint(stack, pltpu.HBM), pltpu.with_memory_space_constraint(flat, pltpu.HBM))


def next_partials(distances, patches, weights, shape, before):
    vmem, unread = pl.BlockSpec(memory_space=pltpu.VMEM), pl.BlockSpec(memory_space=pl.ANY)
    return pl.pallas_call(
        functools.partial(next_kernel, distances),
        in_specs=[vmem, vmem] + [unread] * len(before),
        out_specs=vmem,
        out_shape=jax.ShapeDtypeStruct((2, len(distances), *shape), jnp.float32),
        compiler_params=pltpu.CompilerParams(vmem_limit_bytes=24 * 2**20),
        cost_estimate=kernel_cost(patches.shape[0], shape, len(distances)),
        name="partials_" + "_".join(map(str, distances)),
    )(patches, weights, *before)


def conv_halving(stack, flat, layer_bias):
    shape = stack.shape
    size = lax.axis_size(AXIS)

    def swap(value, bits):
        return lax.ppermute(value, AXIS, [(i, i ^ bits) for i in range(size)])

    def wide(value):
        return value.astype(jnp.float32)

    def core_sums(distances, parts, out):
        sums = {}
        for part in parts:
            first = distances.index(part[0])
            came = swap(out[1, first : first + len(part)].astype(SENT), 1)
            for k, d in enumerate(part):
                sums[d] = out[0, first + k] + wide(came[k])
        return sums

    def across(sums, bit):
        return wide(swap(sums.astype(SENT), 2 * bit))

    odd, even, near = (7, 5), (6, 4), (3, 1, 2, 0)
    patches, odd_out, weights = first_partials(odd, stack, flat)
    even_out = next_partials(even, patches, weights, shape, (odd_out,))
    sums = core_sums(odd, (odd,), odd_out)
    sums.update(core_sums(even, (even,), even_out))
    near_out = next_partials(near, patches, weights, shape, (even_out, sums[7]))
    sums.update(core_sums(near, ((3,), (1, 2), (0,)), near_out))
    came5 = across(sums[5], 1)
    came6 = across(sums[6] + across(sums[7], 1), 2)
    came4 = across(sums[4] + came5 + came6, 4)
    came2 = across(sums[2] + across(sums[3], 1), 2)
    came1 = across(sums[1], 1)
    total = sums[0] + came4 + came2 + came1
    return (wide(stack) + jnp.maximum(total + layer_bias[:, None], 0.0)).astype(jnp.bfloat16)


def local(size, maps, kernels, bias):
    for layer in range(kernels.shape[0]):
        owned = maps.shape[1]
        flat = kernels[layer].reshape(9 * owned, kernels.shape[3])
        if size == 16 and owned % 64 == 0 and maps.shape[2] % 128 == 0 and kernels.shape[3] == size * owned:
            maps = conv_halving(maps, flat, bias[layer])
        else:
            maps = conv_plain(maps, flat, bias[layer])
    return maps


def solution(mesh):
    in_specs = (P("groups", AXIS, None), P(None, None, AXIS, None), P(None, AXIS))
    out_specs = P("groups", AXIS, None)
    return jax.shard_map(
        functools.partial(local, mesh.shape[AXIS]), mesh=mesh, in_specs=in_specs, out_specs=out_specs, check_vma=False
    )
```
